512 devices in a mesh: ctx: 128 (over z_lo, y, x), tp: 4 (over z_hi, core).
Axes of the slice: x: 4, y: 8, z: 8 (z_hi: 2, z_lo: 4; z = z_hi * 4 + z_lo), core: 2. Of those that a mesh axis runs over, the one named last changes fastest.
Arguments:
- hyena_inputs: bfloat16 [3, 16384, 4096], P(None, 'ctx', 'tp'), may hold values from -6 to 6
- filters: float32 [128, 4096], P('tp'), may hold values from -1.25 to 1.25
- skip_bias: float32 [4096], P('tp'), may hold values from -4 to 4
- queries: bfloat16 [16384, 4096], P('ctx', 'tp'), may hold values from -8 to 8
- keys_values: bfloat16 [2, 16384, 4096], P(None, 'ctx', 'tp'), may hold values from -8 to 8
- doc_start: int32 [16384], P('ctx'), may hold values from 0 to 16383, as said below
Outputs:
- hyena_out: bfloat16 [16384, 4096], P('ctx', 'tp')
- attention_out: bfloat16 [16384, 4096], P('ctx', 'tp')
- log_totals: float32 [32, 16384], P('tp', 'ctx')
The draws below stay inside these ranges and needn't reach their ends.
Inputs may be any that keep to these rules, and one draw needn't show every extreme that they name: doc_start[t] <= t; doc_start is non-decreasing, equal within a document and equal to t at a document's first base; no document is longer than 896 bases and one has exactly 896; the last base forms a document of its own.
All inputs are finite; a program needn't handle non-finite values.
Results may differ from the reference program's by a relative error of at most 0.009.
Values may be sent and summed in bfloat16 or wider, within the bound.
A program may use at most 128 MiB of HBM per device.

```python
import math
import jax
import jax.numpy as jnp
from jax import lax

C = 4096
AH = 32
HD = 128
FLEN = 128
TOK_DEV = 128
HOPS = 7
DOC_MAX = 896
TOKENS = 16384


def draw_queries(key, part):
    key = jax.random.fold_in(key, 11)
    drawn = jnp.clip(jax.random.normal(key, (TOKENS, AH * HD), jnp.float32), -6.0, 6.0)
    return drawn.astype(jnp.bfloat16)


def draw_keys_values(key, part):
    key = jax.random.fold_in(key, 13)
    first_key, second_key = jax.random.split(key)
    key_rows = jnp.clip(jax.random.normal(first_key, (TOKENS, AH * HD), jnp.float32), -6.0, 6.0)
    value_rows = jnp.clip(jax.random.normal(second_key, (TOKENS, AH * HD), jnp.float32), -6.0, 6.0)
    return jnp.stack([key_rows, value_rows]).astype(jnp.bfloat16)


def draw_doc_start(key, part):
    key = jax.random.fold_in(key, 17)
    keys = jax.random.split(key, 4)
    places = jnp.arange(TOKENS, dtype=jnp.int32)
    block_count = TOKENS // TOK_DEV
    region_block = jax.random.randint(keys[0], (), 0, block_count - HOPS, dtype=jnp.int32)
    region_offset = jax.random.randint(keys[1], (), TOK_DEV // 4, 3 * TOK_DEV // 4 + 1, dtype=jnp.int32)
    region_start = region_block * TOK_DEV + region_offset
    region_end = region_start + DOC_MAX

    def chain_starts(subkey, anchor):
        lengths = jax.random.randint(subkey, (TOKENS,), 1, DOC_MAX + 1, dtype=jnp.int32)
        starts = jnp.cumsum(lengths).astype(jnp.int32) - lengths
        relative = jnp.maximum(places - anchor, 0)
        which = jnp.searchsorted(starts, relative, side='right').astype(jnp.int32) - 1
        return anchor + starts[which]
    earlier = chain_starts(keys[2], jnp.int32(0))
    later = chain_starts(keys[3], region_end)
    result = jnp.where(places < region_start, earlier, jnp.where(places < region_end, region_start, later))
    result = jnp.where(places == TOKENS - 1, places, result)
    return result.astype(jnp.int32)


def block_scale(key, extent, cuts, least, largest):
    factor_of, own = 1.0, jax.random.fold_in(key, 6)
    for position, shards_of in cuts:
        heights = jnp.exp(jax.random.uniform(jax.random.fold_in(own, position), (shards_of,), jnp.float32, least / len(cuts), largest / len(cuts)))
        factor_of = factor_of * jnp.repeat(heights, extent[position] // shards_of).reshape([-1 if axis == position else 1 for axis in range(len(extent))])
    return factor_of


def noise(key, shape, spread, limit, pieces=(), held_as=jnp.bfloat16):
    array = spread * jax.random.normal(key, shape, jnp.float32)
    if pieces:
        array = array * block_scale(key, shape, pieces, -0.22, 0.18)
    return jnp.clip(array, -limit, limit).astype(held_as)


def setup_inputs(seed: int = 0) -> dict:
    key_list = jax.random.split(jax.random.key(seed), 7)
    return {
        "hyena_inputs": noise(key_list[0], (3, TOKENS, C), 1.0, 6.0, ((1, 128), (2, 4))),
        "filters": noise(key_list[1], (FLEN, C), 0.088, 1.25, ((0, 4),), jnp.float32),
        "skip_bias": noise(key_list[2], (C,), 1.0, 4.0, ((0, 4),), jnp.float32),
        "queries": draw_queries(jax.random.fold_in(key_list[6], 71), 0),
        "keys_values": draw_keys_values(jax.random.fold_in(key_list[6], 71), 0),
        "doc_start": draw_doc_start(jax.random.fold_in(key_list[6], 71), 0),
    }


def reference(hyena_inputs, filters, skip_bias, queries, keys_values, doc_start):
    hyena_query = hyena_inputs[0].astype(jnp.float32)
    kv_product = (hyena_inputs[1].astype(jnp.float32) * hyena_inputs[2].astype(jnp.float32)).astype(jnp.bfloat16)
    kv_product = lax.optimization_barrier(kv_product)
    product = kv_product.astype(jnp.float32)
    block_count = TOKENS // TOK_DEV
    padded = jnp.concatenate([jnp.zeros((FLEN - 1, C), jnp.float32), product], axis=0)

    def convolve_block(block_index):
        begin_row = (block_index * TOK_DEV).astype(jnp.int32)
        window = lax.dynamic_slice_in_dim(padded, begin_row, TOK_DEV + FLEN - 1, 0)
        places = begin_row + jnp.arange(TOK_DEV, dtype=jnp.int32)
        starts = lax.dynamic_slice_in_dim(doc_start, begin_row, TOK_DEV, 0)

        def add_tap(tap_index, running):
            shifted = lax.dynamic_slice_in_dim(window, (FLEN - 1 - tap_index).astype(jnp.int32), TOK_DEV, 0)
            weight = lax.dynamic_slice_in_dim(filters, tap_index, 1, 0)
            allowed = (places - tap_index >= starts)[:, None]
            return running + jnp.where(allowed, shifted * weight, 0.0)
        return lax.fori_loop(jnp.int32(0), jnp.int32(FLEN), add_tap, jnp.zeros((TOK_DEV, C), jnp.float32))
    convolved = lax.map(convolve_block, jnp.arange(block_count, dtype=jnp.int32)).reshape(TOKENS, C)
    hyena_out = (hyena_query * (skip_bias[None, :] * product + convolved)).astype(jnp.bfloat16)
    query_heads = queries.astype(jnp.float32).reshape(TOKENS, AH, HD)
    key_heads = keys_values[0].astype(jnp.float32).reshape(TOKENS, AH, HD)
    value_heads = keys_values[1].astype(jnp.float32).reshape(TOKENS, AH, HD)
    reach_rows = HOPS * TOK_DEV
    key_padded = jnp.concatenate([jnp.zeros((reach_rows, AH, HD), jnp.float32), key_heads], axis=0)
    value_padded = jnp.concatenate([jnp.zeros((reach_rows, AH, HD), jnp.float32), value_heads], axis=0)
    score_scale = 1.0 / math.sqrt(HD)

    def attend(block_index):
        begin_row = (block_index * TOK_DEV).astype(jnp.int32)
        query_rows = lax.dynamic_slice_in_dim(query_heads, begin_row, TOK_DEV, 0)
        key_rows = lax.dynamic_slice_in_dim(key_padded, begin_row, reach_rows + TOK_DEV, 0)
        value_rows = lax.dynamic_slice_in_dim(value_padded, begin_row, reach_rows + TOK_DEV, 0)
        places = begin_row + jnp.arange(TOK_DEV, dtype=jnp.int32)
        key_places = begin_row - reach_rows + jnp.arange(reach_rows + TOK_DEV, dtype=jnp.int32)
        starts = lax.dynamic_slice_in_dim(doc_start, begin_row, TOK_DEV, 0)
        allowed = (key_places[None, :] >= starts[:, None]) & (key_places[None, :] <= places[:, None])
        scores = jnp.einsum('thd,khd->htk', query_rows, key_rows) * score_scale
        scores = jnp.where(allowed[None], scores, -jnp.inf)
        row_top = lax.optimization_barrier(jnp.max(scores, axis=2))
        weights = jnp.exp(scores - row_top[:, :, None])
        denominator = lax.optimization_barrier(jnp.sum(weights, axis=2))
        rounded = lax.optimization_barrier(weights.astype(jnp.bfloat16)).astype(jnp.float32)
        mixed = jnp.einsum('htk,khd->thd', rounded, value_rows) / denominator.T[:, :, None]
        return (mixed.astype(jnp.bfloat16), row_top + jnp.log(denominator))
    outputs, totals = lax.map(attend, jnp.arange(block_count, dtype=jnp.int32))
    attention_out = outputs.reshape(TOKENS, AH * HD)
    log_totals = totals.transpose(1, 0, 2).reshape(AH, TOKENS)
    return (hyena_out, attention_out, log_totals)
```

```python
import functools
import math

import jax
import jax.numpy as jnp
from jax import lax
from jax.experimental import pallas as pl
from jax.experimental.pallas import tpu as pltpu
from jax.sharding import PartitionSpec as P

MESH = pl.DeviceIdType.MESH
HD = 128
FLEN = 128
HOPS = 7
ROW = 4
BLK = 128
SHIFTS = 8


def kernel(
    ctx_count,
    tp_count,
    hy_ref,
    filt_ref,
    bias_ref,
    q_ref,
    kv_ref,
    ds_ref,
    hy_out,
    att_out,
    lt_out,
    kvb,
    qb,
    dsb,
    hyv,
    filtv,
    filtb,
    tapb,
    taps,
    halo,
    prod,
    xw,
    xs,
    ob,
    lts,
    ltr,
    send,
    recv,
    local,
):
    ctx = lax.axis_index("ctx")
    tp = lax.axis_index("tp")
    x = ctx % ROW
    row = ctx // ROW
    row_count = ctx_count // ROW
    up = ((row + 1) % row_count) * ROW + x
    down = ((row + row_count - 1) % row_count) * ROW + x
    after = (ctx + 1) % ctx_count
    before = (ctx + ctx_count - 1) % ctx_count
    ch = hy_ref.shape[2]
    wide = q_ref.shape[1] // ROW
    own_heads = wide // HD
    tap_rows = filt_ref.shape[0]

    def mate(d):
        return row * ROW + (x + d) % ROW

    barrier = pltpu.get_barrier_semaphore()
    peers = [(mate(d), tp) for d in (1, 2, 3)] + [(up, tp), (down, tp), (after, tp), (before, tp)]
    peers += [(ctx, (tp + d) % tp_count) for d in range(1, tp_count)]
    for peer in peers:
        pl.semaphore_signal(barrier, inc=1, device_id=peer, device_id_type=MESH)

    copies = {}

    def remote(name, src, dst, peer):
        index = len(copies)
        copies[name] = pltpu.make_async_remote_copy(
            src_ref=src,
            dst_ref=dst,
            send_sem=send.at[index],
            recv_sem=recv.at[index],
            device_id=peer,
            device_id_type=MESH,
        )
        return copies[name]

    filt_in = pltpu.make_async_copy(filt_ref, filtv, local.at[0])
    hy_in = pltpu.make_async_copy(hy_ref, hyv, local.at[1])
    kv_in = pltpu.make_async_copy(
        kv_ref.at[:, :, pl.ds(pl.multiple_of(x * wide, wide), wide)], kvb.at[8 + x], local.at[2]
    )
    q_in = pltpu.make_async_copy(
        q_ref.at[:, pl.ds(pl.multiple_of(x * wide, wide), wide)], qb.at[x], local.at[3]
    )
    ds_in = pltpu.make_async_copy(ds_ref, dsb.at[x], local.at[4])
    filt_in.start()
    hy_in.start()
    ds_in.start()
    kv_in.start()
    q_in.start()
    pl.semaphore_wait(barrier, len(peers))

    own_cols = pl.ds(pl.multiple_of(x * wide, wide), wide)
    remote(("y1", 0), kv_ref.at[:, :, own_cols], kvb.at[4 + x], (up, tp)).start()
    for d in (1, 3, 2):
        cols = pl.ds(pl.multiple_of(((x + d) % ROW) * wide, wide), wide)
        remote(("kv", d), kv_ref.at[:, :, cols], kvb.at[8 + x], (mate(d), tp)).start()
    filt_in.wait()
    filtb[...] = filtv[...].astype(jnp.bfloat16)
    for d in range(1, tp_count):
        other = (tp + d) % tp_count
        cols = pl.ds(pl.multiple_of(other * ch, ch), ch)
        rows = pl.ds(pl.multiple_of(tp * tap_rows, tap_rows), tap_rows)
        remote(("tap", d), filtb.at[:, cols], tapb.at[rows], (ctx, other)).start()
    tap_in = pltpu.make_async_copy(
        filtb.at[:, pl.ds(pl.multiple_of(tp * ch, ch), ch)],
        tapb.at[pl.ds(pl.multiple_of(tp * tap_rows, tap_rows), tap_rows)],
        local.at[5],
    )
    tap_in.start()
    for d in (1, 3, 2):
        cols = pl.ds(pl.multiple_of(((x + d) % ROW) * wide, wide), wide)
        remote(("q", d), q_ref.at[:, cols], qb.at[x], (mate(d), tp)).start()
        remote(("ds", d), ds_ref, dsb.at[x], (mate(d), tp)).start()
    hy_in.wait()
    product = (hyv[1].astype(jnp.float32) * hyv[2].astype(jnp.float32)).astype(jnp.bfloat16)
    prod[...] = product
    remote(("halo", 0), prod, halo, (after, tp)).start()
    xw[pl.ds(BLK, BLK), :] = product.astype(jnp.float32)

    for d in (1, 3, 2):
        copies[("kv", d)].wait_recv()
        slot = (x + ROW - d) % ROW
        remote(("y1", d), kvb.at[8 + slot], kvb.at[4 + slot], (up, tp)).start()

    hops = (0, 1, 3, 2)

    def forward(d):
        copies[("y1", d)].wait_recv()
        slot = (x + ROW - d) % ROW
        onward = remote(("y2", d), kvb.at[4 + slot], kvb.at[slot], (up, tp))

        @pl.when(slot != 0)
        def _():
            onward.start()

    forward(0)

    copies[("halo", 0)].wait_recv()
    xw[pl.ds(0, BLK), :] = halo[...].astype(jnp.float32)
    for b in range(SHIFTS):
        xs[b, pl.ds(8, 2 * BLK - 8), :] = xw[pl.ds(8 - b, 2 * BLK - 8), :]
    forward(1)
    tap_in.wait()
    for d in range(1, tp_count):
        copies[("tap", d)].wait_recv()
    taps[...] = tapb[...].astype(jnp.float32)
    ds_in.wait()
    base = row * ROW * BLK

    def columns_of(i):
        starts = (dsb[i] - base).astype(jnp.float32)
        return jnp.broadcast_to(starts, (BLK, BLK)).T

    place = lax.broadcasted_iota(jnp.int32, (BLK, BLK), 0).astype(jnp.float32)
    reach = place + (x * BLK).astype(jnp.float32) - columns_of(x)

    def conv_tile(c, carry):
        lanes = pl.ds(pl.multiple_of(c * 128, 128), 128)

        def group(a, acc):
            first = pl.multiple_of(BLK - 8 * a, 8)
            group_taps = taps[pl.ds(pl.multiple_of(8 * a, 8), 8), lanes]
            for b in range(SHIFTS):
                lag = 8 * a + b
                term = xs[b, pl.ds(first, BLK), lanes] * group_taps[b : b + 1]
                acc = acc + jnp.where(reach >= lag.astype(jnp.float32), term, 0.0)
            return acc

        acc = lax.fori_loop(0, FLEN // SHIFTS, group, jnp.zeros((BLK, 128), jnp.float32))
        acc = bias_ref[:, lanes] * xw[pl.ds(BLK, BLK), lanes] + acc
        hy_out[:, lanes] = (hyv[0, :, lanes].astype(jnp.float32) * acc).astype(jnp.bfloat16)
        return carry

    lax.fori_loop(0, ch // 256, conv_tile, 0)
    forward(3)
    lax.fori_loop(ch // 256, ch // 128, conv_tile, 0)
    forward(2)

    kv_in.wait()
    q_in.wait()
    for d in (1, 2, 3):
        copies[("q", d)].wait_recv()
        copies[("ds", d)].wait_recv()
    for d in hops:
        slot = (x + ROW - d) % ROW

        @pl.when(slot != 0)
        def _():
            copies[("y2", d)].wait_recv()

    scale = 1.0 / math.sqrt(HD)
    span = (HOPS + 1) * BLK
    for d in (1, 2, 3, 0):
        i = (x + d) % ROW
        starts = jnp.concatenate([columns_of(i)] * (HOPS + 1), axis=1)
        keys_at = lax.broadcasted_iota(jnp.int32, (BLK, span), 1).astype(jnp.float32) + (
            (i - HOPS) * BLK
        ).astype(jnp.float32)
        queries_at = lax.broadcasted_iota(jnp.int32, (BLK, span), 0).astype(jnp.float32) + (
            i * BLK
        ).astype(jnp.float32)
        allowed = (keys_at >= starts) & (keys_at <= queries_at)
        for h in range(own_heads):
            cols = pl.ds(h * HD, HD)
            queries = qb[i, :, cols]
            keys = kvb[pl.ds(i + 1, HOPS + 1), 0, :, cols].reshape(span, HD)
            values = kvb[pl.ds(i + 1, HOPS + 1), 1, :, cols].reshape(span, HD)
            scores = (
                lax.dot_general(
                    queries, keys, (((1,), (1,)), ((), ())), preferred_element_type=jnp.float32
                )
                * scale
            )
            scores = jnp.where(allowed, scores, -1e30)
            top = jnp.max(scores, axis=1, keepdims=True)
            weights = jnp.exp(scores - top)
            total = jnp.sum(weights, axis=1, keepdims=True)
            mixed = jnp.dot(
                weights.astype(jnp.bfloat16), values, preferred_element_type=jnp.float32
            )
            ob[d, :, cols] = (mixed / total).astype(jnp.bfloat16)
            logs = jnp.broadcast_to(top + jnp.log(total), (BLK, BLK)).T
            lts[d, pl.ds(h, 1), :] = logs[0:1, :]
        mine = att_out.at[:, own_cols]
        if d:
            remote(("o", d), ob.at[d], mine, (mate(d), tp)).start()
            remote(("lt", d), lts.at[d], ltr.at[x], (mate(d), tp)).start()
        else:
            o_in = pltpu.make_async_copy(ob.at[0], mine, local.at[6])
            o_in.start()
            ltr[x] = lts[0]
    o_in.wait()
    for d in (1, 2, 3):
        copies[("o", d)].wait_recv()
        copies[("lt", d)].wait_recv()
    for s in range(ROW):
        lt_out[pl.ds(s * own_heads, own_heads), :] = ltr[s, pl.ds(0, own_heads), :]
    for name, copy in copies.items():
        if name[0] == "y2":
            slot = (x + ROW - name[1]) % ROW

            @pl.when(slot != 0)
            def _():
                copy.wait_send()
        else:
            copy.wait_send()


def local_part(ctx_count, tp_count, hyena_inputs, filters, skip_bias, queries, keys_values, doc_start):
    rows, ch = queries.shape
    heads = ch // HD
    wide = ch // ROW
    hbm = pl.BlockSpec(memory_space=pl.ANY)
    vmem = pl.BlockSpec(memory_space=pltpu.VMEM)
    bf16, f32 = jnp.bfloat16, jnp.float32
    return pl.pallas_call(
        functools.partial(kernel, ctx_count, tp_count),
        name="row_exchange",
        out_shape=(
            jax.ShapeDtypeStruct((rows, ch), bf16),
            jax.ShapeDtypeStruct((rows, ch), bf16),
            jax.ShapeDtypeStruct((heads, rows), f32),
        ),
        in_specs=[hbm, hbm, vmem, hbm, hbm, hbm],
        out_specs=(vmem, hbm, vmem),
        scratch_shapes=[
            pltpu.VMEM((3 * ROW, 2, BLK, wide), bf16),
            pltpu.VMEM((ROW, BLK, wide), bf16),
            pltpu.VMEM((ROW, 1, BLK), jnp.int32),
            pltpu.VMEM((3, BLK, ch), bf16),
            pltpu.VMEM(filters.shape, f32),
            pltpu.VMEM(filters.shape, bf16),
            pltpu.VMEM((FLEN, ch), bf16),
            pltpu.VMEM((FLEN, ch), f32),
            pltpu.VMEM((BLK, ch), bf16),
            pltpu.VMEM((BLK, ch), bf16),
            pltpu.VMEM((2 * BLK, ch), f32),
            pltpu.VMEM((SHIFTS, 2 * BLK, ch), f32),
            pltpu.VMEM((ROW, BLK, wide), bf16),
            pltpu.VMEM((ROW, 8, BLK), f32),
            pltpu.VMEM((ROW, 8, BLK), f32),
            pltpu.SemaphoreType.DMA((32,)),
            pltpu.SemaphoreType.DMA((32,)),
            pltpu.SemaphoreType.DMA((8,)),
        ],
        compiler_params=pltpu.CompilerParams(
            collective_id=0, has_side_effects=True, vmem_limit_bytes=48 * 2**20
        ),
    )(hyena_inputs, filters, skip_bias.reshape(1, ch), queries, keys_values, doc_start.reshape(1, rows))


def solution(mesh):
    in_specs = (
        P(None, "ctx", "tp"),
        P("tp", None),
        P("tp"),
        P("ctx", "tp"),
        P(None, "ctx", "tp"),
        P("ctx"),
    )
    out_specs = (P("ctx", "tp"), P("ctx", "tp"), P("tp", "ctx"))
    part = functools.partial(local_part, mesh.shape["ctx"], mesh.shape["tp"])
    return jax.shard_map(part, mesh=mesh, in_specs=in_specs, out_specs=out_specs, check_vma=False)
```

```python
import functools
import math

import jax
import jax.numpy as jnp
from jax import lax
from jax.experimental import pallas as pl
from jax.experimental.pallas import tpu as pltpu
from jax.sharding import PartitionSpec as P

MESH = pl.DeviceIdType.MESH
HD = 128
FLEN = 128
ROW = 4
BLK = 128
HEADS = 2
SHIFTS = 8
FAR = ROW - 1
NONE = -1e30


def kernel(
    ctx_count,
    tp_count,
    hy_ref,
    filt_ref,
    bias_ref,
    q_ref,
    kv_ref,
    ds_ref,
    hy_out,
    att_out,
    lt_out,
    kvb,
    qb,
    dsb,
    o2s,
    o2r,
    l2s,
    l2r,
    o1s,
    o1r,
    l1s,
    l1r,
    o1p,
    l1p,
    o0p,
    l0p,
    ob,
    lts,
    ltr,
    hyv,
    filtv,
    filtb,
    tapb,
    taps,
    halo,
    prod,
    xw,
    xs,
    send,
    recv,
    local,
):
    ctx = lax.axis_index("ctx")
    tp = lax.axis_index("tp")
    x = ctx % ROW
    row = ctx // ROW
    row_count = ctx_count // ROW
    has_up = row < row_count - 1
    has_up2 = row < row_count - 2
    has_down = row > 0
    up = ((row + 1) % row_count) * ROW + x
    down = ((row + row_count - 1) % row_count) * ROW + x
    after = (ctx + 1) % ctx_count
    before = (ctx + ctx_count - 1) % ctx_count
    ch = hy_ref.shape[2]
    tap_rows = filt_ref.shape[0]
    bf16, f32 = jnp.bfloat16, jnp.float32

    def mate(d):
        return row * ROW + (x + d) % ROW

    def head_cols(owner, h):
        return pl.ds(pl.multiple_of((owner * HEADS + h) * HD, HD), HD)

    barrier = pltpu.get_barrier_semaphore()
    peers = [(mate(d), tp) for d in (1, 2, 3)] + [(up, tp), (down, tp), (after, tp), (before, tp)]
    peers += [(ctx, (tp + d) % tp_count) for d in range(1, tp_count)]
    for peer in peers:
        pl.semaphore_signal(barrier, inc=1, device_id=peer, device_id_type=MESH)

    copies = {}
    sending = {}

    def remote(name, src, dst, peer, when=None):
        index = len(copies)
        copy = pltpu.make_async_remote_copy(
            src_ref=src,
            dst_ref=dst,
            send_sem=send.at[index],
            recv_sem=recv.at[index],
            device_id=peer,
            device_id_type=MESH,
        )
        copies[name] = copy
        sending[name] = when
        if when is None:
            copy.start()
        else:
            pl.when(when)(copy.start)

    def arrived(name, when=None):
        if when is None:
            copies[name].wait_recv()
        else:
            pl.when(when)(copies[name].wait_recv)

    filt_in = pltpu.make_async_copy(filt_ref, filtv, local.at[0])
    hy_in = pltpu.make_async_copy(hy_ref, hyv, local.at[1])
    ds_in = pltpu.make_async_copy(ds_ref, dsb.at[0, x], local.at[2])
    q_in = [
        pltpu.make_async_copy(q_ref.at[:, head_cols(x, h)], qb.at[h, 0, x], local.at[3 + h])
        for h in range(HEADS)
    ]
    kv_in = [
        pltpu.make_async_copy(kv_ref.at[:, :, head_cols(x, h)], kvb.at[h, x], local.at[5 + h])
        for h in range(HEADS)
    ]
    filt_in.start()
    for copy in q_in:
        copy.start()
    ds_in.start()
    hy_in.start()
    for copy in kv_in:
        copy.start()

    @pl.when(row == 0)
    def _():
        o2r[...] = jnp.zeros_like(o2r)
        o1r[...] = jnp.zeros_like(o1r)
        l2r[...] = jnp.full_like(l2r, NONE)
        l1r[...] = jnp.full_like(l1r, NONE)

    @pl.when(ctx == 0)
    def _():
        halo[...] = jnp.zeros_like(halo)

    pl.semaphore_wait(barrier, len(peers))

    for h in range(HEADS):
        for d in (1, 3, 2):
            cols = head_cols((x + d) % ROW, h)
            remote(("q", h, d), q_ref.at[:, cols], qb.at[h, 0, x], (mate(d), tp))
    for d in (1, 3, 2):
        remote(("ds", d), ds_ref, dsb.at[0, x], (mate(d), tp))
    filt_in.wait()
    filtb[...] = filtv[...].astype(bf16)
    own_taps = pl.ds(pl.multiple_of(tp * tap_rows, tap_rows), tap_rows)
    for d in range(1, tp_count):
        other = (tp + d) % tp_count
        cols = pl.ds(pl.multiple_of(other * ch, ch), ch)
        remote(("tap", d), filtb.at[:, cols], tapb.at[own_taps], (ctx, other))
    tap_in = pltpu.make_async_copy(
        filtb.at[:, pl.ds(pl.multiple_of(tp * ch, ch), ch)], tapb.at[own_taps], local.at[7]
    )
    tap_in.start()
    for h in range(HEADS):
        for d in (1, 3, 2):
            cols = head_cols((x + d) % ROW, h)
            remote(("kv", h, d), kv_ref.at[:, :, cols], kvb.at[h, x], (mate(d), tp))

    ds_in.wait()
    for d in (1, 3, 2):
        arrived(("ds", d))
    remote("ds1", dsb.at[0], dsb.at[1], (down, tp), has_down)
    for h in range(HEADS):
        q_in[h].wait()
        for d in (1, 3, 2):
            arrived(("q", h, d))
        remote(("q1", h), qb.at[h, 0], qb.at[h, 1], (down, tp), has_down)

    hy_in.wait()
    product = (hyv[1].astype(f32) * hyv[2].astype(f32)).astype(bf16)
    prod[...] = product
    has_after = ctx < ctx_count - 1
    has_before = ctx > 0
    remote("halo", prod, halo, (after, tp), has_after)
    xw[pl.ds(BLK, BLK), :] = product.astype(f32)

    both = has_down & has_up
    arrived("ds1", has_up)
    remote("ds2", dsb.at[1], dsb.at[2], (down, tp), both)
    for h in range(HEADS):
        arrived(("q1", h), has_up)
        remote(
            ("q2", h),
            qb.at[h, 1, pl.ds(0, FAR)],
            qb.at[h, 2, pl.ds(0, FAR)],
            (down, tp),
            both,
        )

    base = row * ROW * BLK
    scale = 1.0 / math.sqrt(HD)

    def attend(h, level, first):
        count = FAR if level == 2 else ROW
        span = (ROW - first) * BLK
        keys = kvb[h, pl.ds(first, ROW - first), 0].reshape(span, HD)
        values = kvb[h, pl.ds(first, ROW - first), 1].reshape(span, HD)
        queries = qb[h, level, pl.ds(0, count)].reshape(count * BLK, HD)
        scores = lax.dot_general(
            keys, queries, (((1,), (1,)), ((), ())), preferred_element_type=f32
        )
        starts = jnp.concatenate([dsb[level, i] for i in range(count)], axis=1) - base
        places = lax.broadcasted_iota(jnp.int32, scores.shape, 0) + first * BLK
        allowed = places >= starts
        if level == 0:
            allowed = allowed & (places <= lax.broadcasted_iota(jnp.int32, scores.shape, 1))
        scores = jnp.where(allowed, scores * scale, NONE)
        top = jnp.max(scores, axis=0, keepdims=True)
        weights = jnp.exp(scores - top)
        total = jnp.sum(weights, axis=0, keepdims=True)
        mixed = lax.dot_general(
            values, weights.astype(bf16), (((0,), (0,)), ((), ())), preferred_element_type=f32
        )
        return mixed / total, top + jnp.log(total)

    def merged(mixed_a, logs_a, mixed_b, logs_b):
        top = jnp.maximum(logs_a, logs_b)
        share_a = jnp.exp(logs_a - top)
        share_b = jnp.exp(logs_b - top)
        total = share_a + share_b
        mixed = mixed_a * (share_a / total) + mixed_b * (share_b / total)
        return mixed, top + jnp.log(total)

    def far_part(h):
        arrived(("q2", h), has_up2)

        @pl.when(has_up2)
        def _():
            mixed, logs = attend(h, 2, 1)
            o2s[h] = mixed.astype(bf16)
            l2s[h] = logs

        remote(("o2", h), o2s.at[h], o2r.at[h], (up, tp), has_up2)
        remote(("l2", h), l2s.at[h], l2r.at[h], (up, tp), has_up2)

    def near_part(h):
        @pl.when(has_up)
        def _():
            mixed, logs = attend(h, 1, 0)
            o1p[h] = mixed
            l1p[h] = logs

    def own_part(h):
        mixed, logs = attend(h, 0, 0)
        o0p[h] = mixed
        l0p[h] = logs

    def pass_on(h):
        came = both
        arrived(("o2", h), came)
        arrived(("l2", h), came)

        @pl.when(has_up)
        def _():
            far, far_logs = o2r[h].astype(f32), l2r[h]
            cut = FAR * BLK
            mixed, logs = merged(o1p[h, :, pl.ds(0, cut)], l1p[h, :, pl.ds(0, cut)], far, far_logs)
            o1s[h, :, pl.ds(0, cut)] = mixed.astype(bf16)
            l1s[h, :, pl.ds(0, cut)] = logs
            o1s[h, :, pl.ds(cut, BLK)] = o1p[h, :, pl.ds(cut, BLK)].astype(bf16)
            l1s[h, :, pl.ds(cut, BLK)] = l1p[h, :, pl.ds(cut, BLK)]

        remote(("o1", h), o1s.at[h], o1r.at[h], (up, tp), has_up)
        remote(("l1", h), l1s.at[h], l1r.at[h], (up, tp), has_up)

    def finish(h):
        arrived(("o1", h), has_down)
        arrived(("l1", h), has_down)
        mixed, logs = merged(o0p[h], l0p[h], o1r[h].astype(f32), l1r[h])
        for i in range(ROW):
            ob[h, i] = mixed[:, i * BLK : (i + 1) * BLK].T.astype(bf16)
            lts[h, i] = logs[:, i * BLK : (i + 1) * BLK]
        for d in (1, 3, 2):
            to = (x + d) % ROW
            remote(("o", h, d), ob.at[h, to], att_out.at[:, head_cols(x, h)], (mate(d), tp))
            remote(("lt", h, d), lts.at[h, to], ltr.at[h, x], (mate(d), tp))
        att_out[:, head_cols(x, h)] = ob[h, x]
        ltr[h, x] = lts[h, x]

    def conv_tile(c, carry):
        lanes = pl.ds(pl.multiple_of(c * 128, 128), 128)
        starts = jnp.broadcast_to((dsb[0, x] - base).astype(f32), (BLK, BLK)).T
        place = lax.broadcasted_iota(jnp.int32, (BLK, BLK), 0).astype(f32)
        reach = place + (x * BLK).astype(f32) - starts

        def group(a, acc):
            first = pl.multiple_of(BLK - 8 * a, 8)
            group_taps = taps[pl.ds(pl.multiple_of(8 * a, 8), 8), lanes]
            for b in range(SHIFTS):
                lag = 8 * a + b
                term = xs[b, pl.ds(first, BLK), lanes] * group_taps[b : b + 1]
                acc = acc + jnp.where(reach >= lag.astype(f32), term, 0.0)
            return acc

        acc = lax.fori_loop(0, FLEN // SHIFTS, group, jnp.zeros((BLK, 128), f32))
        acc = bias_ref[:, lanes] * xw[pl.ds(BLK, BLK), lanes] + acc
        hy_out[:, lanes] = (hyv[0, :, lanes].astype(f32) * acc).astype(bf16)
        return carry

    tiles = ch // 128

    def convolve(first, last):
        lax.fori_loop(first, last, conv_tile, 0)

    arrived("ds2", has_up2)
    for h in range(HEADS):
        kv_in[h].wait()
        for d in (1, 3, 2):
            arrived(("kv", h, d))
        far_part(h)
        near_part(h)
    for h in range(HEADS):
        own_part(h)
    tap_in.wait()
    for d in range(1, tp_count):
        arrived(("tap", d))
    taps[...] = tapb[...].astype(f32)
    arrived("halo", has_before)
    xw[pl.ds(0, BLK), :] = halo[...].astype(f32)
    for b in range(SHIFTS):
        xs[b, pl.ds(8, 2 * BLK - 8), :] = xw[pl.ds(8 - b, 2 * BLK - 8), :]
    pass_on(0)
    convolve(0, tiles // 4)
    pass_on(1)
    convolve(tiles // 4, tiles // 2)
    finish(0)
    convolve(tiles // 2, 3 * tiles // 4)
    finish(1)
    convolve(3 * tiles // 4, tiles)
    for h in range(HEADS):
        for d in (1, 3, 2):
            arrived(("o", h, d))
            arrived(("lt", h, d))
    for s in range(ROW):
        for h in range(HEADS):
            lt_out[pl.ds(s * HEADS + h, 1), :] = ltr[h, s]
    for name, copy in copies.items():
        if sending[name] is None:
            copy.wait_send()
        else:
            pl.when(sending[name])(copy.wait_send)


def local_part(ctx_count, tp_count, hyena_inputs, filters, skip_bias, queries, keys_values, doc_start):
    rows, ch = queries.shape
    heads = ch // HD
    wide = ROW * BLK
    hbm = pl.BlockSpec(memory_space=pl.ANY)
    vmem = pl.BlockSpec(memory_space=pltpu.VMEM)
    bf16, f32 = jnp.bfloat16, jnp.float32
    return pl.pallas_call(
        functools.partial(kernel, ctx_count, tp_count),
        name="row_exchange",
        out_shape=(
            jax.ShapeDtypeStruct((rows, ch), bf16),
            jax.ShapeDtypeStruct((rows, ch), bf16),
            jax.ShapeDtypeStruct((heads, rows), f32),
        ),
        in_specs=[hbm, hbm, vmem, hbm, hbm, hbm],
        out_specs=(vmem, vmem, vmem),
        scratch_shapes=[
            pltpu.VMEM((HEADS, ROW, 2, BLK, HD), bf16),
            pltpu.VMEM((HEADS, 3, ROW, BLK, HD), bf16),
            pltpu.VMEM((3, ROW, 1, BLK), jnp.int32),
            pltpu.VMEM((HEADS, HD, FAR * BLK), bf16),
            pltpu.VMEM((HEADS, HD, FAR * BLK), bf16),
            pltpu.VMEM((HEADS, 1, FAR * BLK), f32),
            pltpu.VMEM((HEADS, 1, FAR * BLK), f32),
            pltpu.VMEM((HEADS, HD, wide), bf16),
            pltpu.VMEM((HEADS, HD, wide), bf16),
            pltpu.VMEM((HEADS, 1, wide), f32),
            pltpu.VMEM((HEADS, 1, wide), f32),
            pltpu.VMEM((HEADS, HD, wide), f32),
            pltpu.VMEM((HEADS, 1, wide), f32),
            pltpu.VMEM((HEADS, HD, wide), f32),
            pltpu.VMEM((HEADS, 1, wide), f32),
            pltpu.VMEM((HEADS, ROW, BLK, HD), bf16),
            pltpu.VMEM((HEADS, ROW, 1, BLK), f32),
            pltpu.VMEM((HEADS, ROW, 1, BLK), f32),
            pltpu.VMEM((3, BLK, ch), bf16),
            pltpu.VMEM(filters.shape, f32),
            pltpu.VMEM(filters.shape, bf16),
            pltpu.VMEM((FLEN, ch), bf16),
            pltpu.VMEM((FLEN, ch), f32),
            pltpu.VMEM((BLK, ch), bf16),
            pltpu.VMEM((BLK, ch), bf16),
            pltpu.VMEM((2 * BLK, ch), f32),
            pltpu.VMEM((SHIFTS, 2 * BLK, ch), f32),
            pltpu.SemaphoreType.DMA((48,)),
            pltpu.SemaphoreType.DMA((48,)),
            pltpu.SemaphoreType.DMA((8,)),
        ],
        compiler_params=pltpu.CompilerParams(
            collective_id=0, has_side_effects=True, vmem_limit_bytes=63 * 2**20
        ),
    )(hyena_inputs, filters, skip_bias.reshape(1, ch), queries, keys_values, doc_start.reshape(1, rows))


def solution(mesh):
    in_specs = (
        P(None, "ctx", "tp"),
        P("tp", None),
        P("tp"),
        P("ctx", "tp"),
        P(None, "ctx", "tp"),
        P("ctx"),
    )
    out_specs = (P("ctx", "tp"), P("ctx", "tp"), P("tp", "ctx"))
    part = functools.partial(local_part, mesh.shape["ctx"], mesh.shape["tp"])
    return jax.shard_map(part, mesh=mesh, in_specs=in_specs, out_specs=out_specs, check_vma=False)
```

```python
import functools
import math

import jax
import jax.numpy as jnp
from jax import lax
from jax.experimental import pallas as pl
from jax.experimental.pallas import tpu as pltpu
from jax.sharding import PartitionSpec as P

MESH = pl.DeviceIdType.MESH
HD = 128
FLEN = 128
ROW = 4
BLK = 128
CORES = 2
PLANES = 4
PARTNER = (2, 1, 3, 0)
HEADS = 2
SHIFTS = 8
NONE = -1e30
NOTE = 16


def kernel(
    ctx_count,
    tp_count,
    hy_ref,
    filt_ref,
    bias_ref,
    q_ref,
    kv_ref,
    ds_ref,
    hy_out,
    att_out,
    lt_out,
    kvb,
    qb,
    dsb,
    sent,
    came,
    hyv,
    filtv,
    filtb,
    tapb,
    taps,
    halo,
    prod,
    early,
    late,
    earlys,
    lates,
    convolved,
    biasv,
    send,
    recv,
    local,
    ready,
):
    ctx = lax.axis_index("ctx")
    tp = lax.axis_index("tp")
    x = ctx % ROW
    row = ctx // ROW
    row_count = ctx_count // ROW
    plane = ctx_count // PLANES
    has_up = row < row_count - 1
    has_down = row > 0
    up = ((row + 1) % row_count) * ROW + x
    down = ((row + row_count - 1) % row_count) * ROW + x
    after = (ctx + 1) % ctx_count
    ch = hy_ref.shape[2]
    tap_rows = filt_ref.shape[0]
    bf16, f32 = jnp.bfloat16, jnp.float32

    def mate(d):
        return row * ROW + (x + d) % ROW

    def head_cols(owner, h):
        return pl.ds(pl.multiple_of((owner * HEADS + h) * HD, HD), HD)

    level = ctx // plane
    low = tp < CORES
    partner = 0
    for mine in range(PLANES):
        theirs = jnp.where(low, PARTNER[mine], PARTNER.index(mine))
        partner = jnp.where(level == mine, theirs, partner)
    mirrored = partner * plane + ctx % plane

    def holder(other):
        return jnp.where(other // CORES == tp // CORES, ctx, mirrored)

    def higher(d):
        return ((row + 1) % row_count) * ROW + (x + d) % ROW

    def lower(d):
        return ((row + row_count - 1) % row_count) * ROW + (x + d) % ROW

    barrier = pltpu.get_barrier_semaphore()

    def greet(peer):
        pl.semaphore_signal(barrier, inc=1, device_id=peer, device_id_type=MESH)

    for d in range(1, ROW):
        greet((mate(d), tp))
    for other in range(1, tp_count):

        @pl.when(other > tp)
        def _():
            greet((holder(other), other))

    @pl.when(has_up)
    def _():
        for d in range(ROW):
            greet((higher(d), tp))

    @pl.when(has_down)
    def _():
        for d in range(ROW):
            greet((lower(d), tp))

    greetings = ROW - 1 + tp + ROW * (has_up.astype(jnp.int32) + has_down.astype(jnp.int32))

    copies = {}
    sending = {}

    def remote(name, src, dst, peer, when=None):
        index = len(copies)
        copy = pltpu.make_async_remote_copy(
            src_ref=src,
            dst_ref=dst,
            send_sem=send.at[index],
            recv_sem=recv.at[index],
            device_id=peer,
            device_id_type=MESH,
        )
        copies[name] = copy
        sending[name] = when
        if when is None:
            copy.start()
        else:
            pl.when(when)(copy.start)

    def arrived(name, when=None):
        if when is None:
            copies[name].wait_recv()
        else:
            pl.when(when)(copies[name].wait_recv)

    filt_in = pltpu.make_async_copy(filt_ref, filtv, local.at[0])
    hy_in = pltpu.make_async_copy(hy_ref, hyv, local.at[1])
    ds_in = pltpu.make_async_copy(ds_ref, dsb.at[0, x], local.at[2])
    q_in = [
        pltpu.make_async_copy(q_ref.at[:, head_cols(x, h)], qb.at[h, 0, x], local.at[3 + h])
        for h in range(HEADS)
    ]
    kv_in = [
        pltpu.make_async_copy(kv_ref.at[:, :, head_cols(x, h)], kvb.at[h, ROW + x], local.at[5 + h])
        for h in range(HEADS)
    ]
    filt_in.start()
    for copy in q_in:
        copy.start()
    ds_in.start()
    hy_in.start()
    bias_in = pltpu.make_async_copy(bias_ref, biasv, local.at[8])
    bias_in.start()
    for copy in kv_in:
        copy.start()

    @pl.when(row == 0)
    def _():
        note = lax.broadcasted_iota(jnp.int32, (NOTE, BLK), 0)
        for h in range(HEADS):
            for s in range(ROW):
                came[1, h, s, pl.ds(0, HD), :] = jnp.zeros((HD, BLK), bf16)
                came[1, h, s, pl.ds(HD, NOTE), :] = jnp.where(note == 0, NONE, 0.0).astype(bf16)
        for h in range(HEADS):
            kvb[h, pl.ds(0, ROW)] = jnp.zeros((ROW, 2, BLK, HD), bf16)

    @pl.when(ctx == 0)
    def _():
        halo[...] = jnp.zeros_like(halo)

    pl.semaphore_wait(barrier, greetings)
    for other in range(tp_count - 1):

        @pl.when(other < tp)
        def _():
            pl.semaphore_signal(
                ready.at[tp], inc=1, device_id=(holder(other), other), device_id_type=MESH
            )

    def slot(d):
        return (x + ROW - d) % ROW

    def send_queries(h):
        for d in (1, 3, 2):
            cols = head_cols((x + d) % ROW, h)
            remote(("q", h, d), q_ref.at[:, cols], qb.at[h, 0, x], (mate(d), tp))
        remote(("qd", h, 0), q_ref.at[:, head_cols(x, h)], qb.at[h, 1, x], (down, tp), has_down)

    def send_keys(h):
        for d in (1, 3, 2):
            cols = head_cols((x + d) % ROW, h)
            remote(("kv", h, d), kv_ref.at[:, :, cols], kvb.at[h, ROW + x], (mate(d), tp))
        remote(
            ("ku", h, 0),
            kv_ref.at[:, :, head_cols(x, h)],
            kvb.at[h, x],
            (up, tp),
            has_up & (x != 0),
        )

    def queries_down(h, d):
        arrived(("q", h, d))
        remote(("qd", h, d), qb.at[h, 0, slot(d)], qb.at[h, 1, slot(d)], (down, tp), has_down)

    def keys_up(h, d):
        arrived(("kv", h, d))
        remote(
            ("ku", h, d),
            kvb.at[h, ROW + slot(d)],
            kvb.at[h, slot(d)],
            (up, tp),
            has_up & (slot(d) != 0),
        )

    send_queries(0)
    send_keys(0)
    for d in (1, 3, 2):
        remote(("ds", d), ds_ref, dsb.at[0, x], (mate(d), tp))
    filt_in.wait()
    filtb[...] = filtv[...].astype(bf16)
    own_taps = pl.ds(pl.multiple_of(tp * tap_rows, tap_rows), tap_rows)
    for d in range(1, tp_count):
        other = (tp + d) % tp_count
        cols = pl.ds(pl.multiple_of(other * ch, ch), ch)
        remote(("tap", d), filtb.at[:, cols], tapb.at[own_taps], (holder(other), other), other < tp)
        sending[("tap", d)] = None
    tap_in = pltpu.make_async_copy(
        filtb.at[:, pl.ds(pl.multiple_of(tp * ch, ch), ch)], tapb.at[own_taps], local.at[7]
    )
    tap_in.start()
    for d in (1, 3, 2):
        queries_down(0, d)
    ds_in.wait()
    for d in (1, 3, 2):
        arrived(("ds", d))
    remote("ds1", dsb.at[0], dsb.at[1], (down, tp), has_down)
    keys_up(0, 1)
    keys_up(0, 3)
    send_queries(1)
    keys_up(0, 2)
    send_keys(1)

    hy_in.wait()
    product = (hyv[1].astype(f32) * hyv[2].astype(f32)).astype(bf16)
    prod[...] = product
    late[pl.ds(0, SHIFTS), :] = jnp.zeros((SHIFTS, ch), f32)
    late[pl.ds(SHIFTS, BLK), :] = product.astype(f32)
    for b in range(SHIFTS):
        lates[b] = late[pl.ds(SHIFTS - b, BLK), :]

    for d in (1, 3, 2):
        queries_down(1, d)
    for d in (1, 3, 2):
        keys_up(1, d)
    for d in range(1, tp_count):
        other = (tp + d) % tp_count

        @pl.when(other > tp)
        def _():
            pl.semaphore_wait(ready.at[other], 1)
            copies[("tap", d)].start()

    remote("halo", prod, halo, (after, tp), ctx < ctx_count - 1)

    base = row * ROW * BLK
    scale = 1.0 / math.sqrt(HD)

    def attend(h, level, first):
        span = (2 * ROW - first) * BLK
        keys = kvb[h, pl.ds(first, 2 * ROW - first), 0].reshape(span, HD)
        values = kvb[h, pl.ds(first, 2 * ROW - first), 1].reshape(span, HD)
        queries = qb[h, level].reshape(ROW * BLK, HD)
        scores = lax.dot_general(
            keys, queries, (((1,), (1,)), ((), ())), preferred_element_type=f32
        )
        starts = jnp.concatenate([dsb[level, i] for i in range(ROW)], axis=1) - base
        places = lax.broadcasted_iota(jnp.int32, scores.shape, 0) + (first - ROW) * BLK
        allowed = places >= starts
        if level == 0:
            allowed = allowed & (places <= lax.broadcasted_iota(jnp.int32, scores.shape, 1))
        scores = jnp.where(allowed, scores * scale, NONE)
        top = jnp.max(scores, axis=0, keepdims=True)
        weights = jnp.exp(scores - top)
        total = jnp.sum(weights, axis=0, keepdims=True)
        mixed = lax.dot_general(
            values, weights.astype(bf16), (((0,), (0,)), ((), ())), preferred_element_type=f32
        )
        return mixed / total, top + jnp.log(total)

    def merged(mixed_a, logs_a, mixed_b, logs_b):
        top = jnp.maximum(logs_a, logs_b)
        share_a = jnp.exp(logs_a - top)
        share_b = jnp.exp(logs_b - top)
        total = share_a + share_b
        mixed = mixed_a * (share_a / total) + mixed_b * (share_b / total)
        return mixed, top + jnp.log(total)

    def stage(level, h, mixed, logs):
        first = logs.astype(bf16).astype(f32)
        second = (logs - first).astype(bf16).astype(f32)
        third = logs - first - second
        place = lax.broadcasted_iota(jnp.int32, (NOTE, BLK), 0)
        for i in range(ROW):
            cols = slice(i * BLK, (i + 1) * BLK)
            sent[level, h, i, pl.ds(0, HD), :] = mixed[:, cols].astype(bf16)
            terms = jnp.where(
                place == 0,
                first[:, cols],
                jnp.where(place == 1, second[:, cols], jnp.where(place == 2, third[:, cols], 0.0)),
            )
            sent[level, h, i, pl.ds(HD, NOTE), :] = terms.astype(bf16)

    def own_part(h):
        q_in[h].wait()
        kv_in[h].wait()
        stage(0, h, *attend(h, 0, ROW))
        for d in (1, 3, 2):
            to = (x + d) % ROW
            remote(("o0", h, d), sent.at[0, h, to], came.at[0, h, x], (mate(d), tp))
        came[0, h, x] = sent[0, h, x]

    def earlier_part(h):
        for d in range(ROW):
            arrived(("qd", h, d), has_up)
            arrived(("ku", h, d), has_down & (slot(d) != 0))

        @pl.when(has_up)
        def _():
            stage(1, h, *attend(h, 1, 1))

        for d in (0, 1, 3, 2):
            to = (x + d) % ROW
            remote(("o1", h, d), sent.at[1, h, to], came.at[1, h, x], (higher(d), tp), has_up)

    def finish(h, s):
        own, earlier = came[0, h, s], came[1, h, s]

        def logs_of(tile):
            note = tile[HD:].astype(f32)
            return note[0:1] + note[1:2] + note[2:3]

        mixed, logs = merged(
            own[:HD].astype(f32), logs_of(own), earlier[:HD].astype(f32), logs_of(earlier)
        )
        head = s * HEADS + h
        att_out[:, pl.ds(head * HD, HD)] = mixed.T.astype(bf16)
        lt_out[pl.ds(head, 1), :] = logs

    groups = BLK // SHIFTS

    def reach_tiles():
        starts = jnp.broadcast_to((dsb[0, x] - base).astype(f32), (BLK, BLK)).T
        place = lax.broadcasted_iota(jnp.int32, (BLK, BLK), 0).astype(f32)
        reach = place + (x * BLK).astype(f32) - starts
        return [reach[SHIFTS * k : SHIFTS * (k + 1)] for k in range(groups)]

    def add_taps(acc, source, lanes, first_of, last_of, row_of):
        reach = reach_tiles()
        for a in range(groups):
            group_taps = taps[pl.ds(SHIFTS * a, SHIFTS), lanes]
            for b in range(SHIFTS):
                weight = jnp.broadcast_to(group_taps[b : b + 1], (SHIFTS, BLK))
                for k in range(first_of(a), last_of(a)):
                    term = source[b, pl.ds(SHIFTS * row_of(k, a), SHIFTS), lanes] * weight
                    acc[k] = acc[k] + jnp.where(reach[k] >= SHIFTS * a + b, term, 0.0)

    def late_tile(c, carry):
        lanes = pl.ds(pl.multiple_of(c * 128, 128), 128)
        acc = [jnp.zeros((SHIFTS, 128), f32) for _ in range(groups)]
        add_taps(acc, lates, lanes, lambda a: a, lambda a: groups, lambda k, a: k - a)
        for k in range(groups):
            convolved[pl.ds(SHIFTS * k, SHIFTS), lanes] = acc[k]
        return carry

    def early_tile(c, carry):
        lanes = pl.ds(pl.multiple_of(c * 128, 128), 128)
        acc = [convolved[pl.ds(SHIFTS * k, SHIFTS), lanes] for k in range(groups)]
        add_taps(acc, earlys, lanes, lambda a: 0, lambda a: a + 1, lambda k, a: groups + k - a)
        total = jnp.concatenate(acc, axis=0)
        total = biasv[:, lanes] * late[pl.ds(SHIFTS, BLK), lanes] + total
        hy_out[:, lanes] = (hyv[0, :, lanes].astype(f32) * total).astype(bf16)
        return carry

    tiles = ch // 128

    own_part(0)
    own_part(1)
    tap_in.wait()
    for d in range(1, tp_count):
        arrived(("tap", d))
    taps[...] = tapb[...].astype(f32)
    arrived("ds1", has_up)
    lax.fori_loop(0, tiles // 2, late_tile, 0)
    earlier_part(0)
    lax.fori_loop(tiles // 2, tiles, late_tile, 0)
    earlier_part(1)
    arrived("halo", ctx > 0)
    early[pl.ds(0, BLK), :] = halo[...].astype(f32)
    early[pl.ds(BLK, SHIFTS), :] = jnp.zeros((SHIFTS, ch), f32)
    for b in range(SHIFTS):
        earlys[b, pl.ds(SHIFTS, BLK), :] = early[pl.ds(SHIFTS - b, BLK), :]
    bias_in.wait()
    lax.fori_loop(0, tiles, early_tile, 0)
    for h in range(HEADS):
        for d in (1, 3, 2):
            arrived(("o0", h, d))
        for d in (0, 1, 3, 2):
            arrived(("o1", h, d), has_down)
        for s in range(ROW):
            finish(h, s)
    for name, copy in copies.items():
        if sending[name] is None:
            copy.wait_send()
        else:
            pl.when(sending[name])(copy.wait_send)


def local_part(ctx_count, tp_count, hyena_inputs, filters, skip_bias, queries, keys_values, doc_start):
    rows, ch = queries.shape
    heads = ch // HD
    hbm = pl.BlockSpec(memory_space=pltpu.HBM)
    vmem = pl.BlockSpec(memory_space=pltpu.VMEM)

    def in_hbm(array):
        return pltpu.with_memory_space_constraint(array, pltpu.HBM)

    bf16, f32 = jnp.bfloat16, jnp.float32
    return pl.pallas_call(
        functools.partial(kernel, ctx_count, tp_count),
        name="row_exchange",
        out_shape=(
            jax.ShapeDtypeStruct((rows, ch), bf16),
            jax.ShapeDtypeStruct((rows, ch), bf16),
            jax.ShapeDtypeStruct((heads, rows), f32),
        ),
        in_specs=[hbm] * 6,
        out_specs=(vmem, vmem, vmem),
        scratch_shapes=[
            pltpu.VMEM((HEADS, 2 * ROW, 2, BLK, HD), bf16),
            pltpu.VMEM((HEADS, 2, ROW, BLK, HD), bf16),
            pltpu.VMEM((2, ROW, 1, BLK), jnp.int32),
            pltpu.VMEM((2, HEADS, ROW, HD + NOTE, BLK), bf16),
            pltpu.VMEM((2, HEADS, ROW, HD + NOTE, BLK), bf16),
            pltpu.VMEM((3, BLK, ch), bf16),
            pltpu.VMEM(filters.shape, f32),
            pltpu.VMEM(filters.shape, bf16),
            pltpu.VMEM((FLEN, ch), bf16),
            pltpu.VMEM((FLEN, ch), f32),
            pltpu.VMEM((BLK, ch), bf16),
            pltpu.VMEM((BLK, ch), bf16),
            pltpu.VMEM((BLK + SHIFTS, ch), f32),
            pltpu.VMEM((SHIFTS + BLK, ch), f32),
            pltpu.VMEM((SHIFTS, BLK + SHIFTS, ch), f32),
            pltpu.VMEM((SHIFTS, BLK, ch), f32),
            pltpu.VMEM((BLK, ch), f32),
            pltpu.VMEM((1, ch), f32),
            pltpu.SemaphoreType.DMA((56,)),
            pltpu.SemaphoreType.DMA((56,)),
            pltpu.SemaphoreType.DMA((9,)),
            pltpu.SemaphoreType.REGULAR((tp_count,)),
        ],
        compiler_params=pltpu.CompilerParams(
            collective_id=0, has_side_effects=True, vmem_limit_bytes=40 * 2**20
        ),
    )(
        in_hbm(hyena_inputs),
        in_hbm(filters),
        in_hbm(skip_bias.reshape(1, ch)),
        in_hbm(queries),
        in_hbm(keys_values),
        in_hbm(doc_start.reshape(1, rows)),
    )


def solution(mesh):
    in_specs = (
        P(None, "ctx", "tp"),
        P("tp", None),
        P("tp"),
        P("ctx", "tp"),
        P(None, "ctx", "tp"),
        P("ctx"),
    )
    out_specs = (P("ctx", "tp"), P("ctx", "tp"), P("tp", "ctx"))
    part = functools.partial(local_part, mesh.shape["ctx"], mesh.shape["tp"])
    return jax.shard_map(part, mesh=mesh, in_specs=in_specs, out_specs=out_specs, check_vma=False)
```

```python
import functools
import math

import jax
import jax.numpy as jnp
from jax import lax
from jax.experimental import pallas as pl
from jax.experimental.pallas import tpu as pltpu
from jax.sharding import PartitionSpec as P

MESH = pl.DeviceIdType.MESH
HD = 128
FLEN = 128
ROW = 4
BLK = 128
CORES = 2
PLANES = 4
PARTNER = (2, 1, 3, 0)
HEADS = 2
SHIFTS = 8
NONE = -1e30
NOTE = 16


def kernel(
    ctx_count,
    tp_count,
    hy_ref,
    filt_ref,
    bias_ref,
    q_ref,
    kv_ref,
    ds_ref,
    hy_out,
    att_out,
    lt_out,
    kvb,
    qb,
    dsb,
    sent,
    came,
    hyv,
    filtv,
    filtb,
    tapb,
    taps,
    halo,
    prod,
    early,
    late,
    earlys,
    lates,
    convolved,
    biasv,
    send,
    recv,
    local,
    ready,
):
    ctx = lax.axis_index("ctx")
    tp = lax.axis_index("tp")
    x = ctx % ROW
    row = ctx // ROW
    row_count = ctx_count // ROW
    plane = ctx_count // PLANES
    has_up = row < row_count - 1
    has_down = row > 0
    up = ((row + 1) % row_count) * ROW + x
    down = ((row + row_count - 1) % row_count) * ROW + x
    after = (ctx + 1) % ctx_count
    ch = hy_ref.shape[2]
    tap_rows = filt_ref.shape[0]
    bf16, f32 = jnp.bfloat16, jnp.float32

    def mate(d):
        return row * ROW + (x + d) % ROW

    def head_cols(owner, h):
        return pl.ds(pl.multiple_of((owner * HEADS + h) * HD, HD), HD)

    level = ctx // plane
    low = tp < CORES
    partner = 0
    for mine in range(PLANES):
        theirs = jnp.where(low, PARTNER[mine], PARTNER.index(mine))
        partner = jnp.where(level == mine, theirs, partner)
    mirrored = partner * plane + ctx % plane

    def holder(other):
        return jnp.where(other // CORES == tp // CORES, ctx, mirrored)

    def higher(d):
        return ((row + 1) % row_count) * ROW + (x + d) % ROW

    def lower(d):
        return ((row + row_count - 1) % row_count) * ROW + (x + d) % ROW

    barrier = pltpu.get_barrier_semaphore()

    def greet(peer):
        pl.semaphore_signal(barrier, inc=1, device_id=peer, device_id_type=MESH)

    for d in range(1, ROW):
        greet((mate(d), tp))
    for other in range(1, tp_count):

        @pl.when(other > tp)
        def _():
            greet((holder(other), other))

    @pl.when(has_up)
    def _():
        for d in range(ROW):
            greet((higher(d), tp))

    @pl.when(has_down)
    def _():
        for d in range(ROW):
            greet((lower(d), tp))

    greetings = ROW - 1 + tp + ROW * (has_up.astype(jnp.int32) + has_down.astype(jnp.int32))

    copies = {}
    sending = {}

    def remote(name, src, dst, peer, when=None):
        index = len(copies)
        copy = pltpu.make_async_remote_copy(
            src_ref=src,
            dst_ref=dst,
            send_sem=send.at[index],
            recv_sem=recv.at[index],
            device_id=peer,
            device_id_type=MESH,
        )
        copies[name] = copy
        sending[name] = when
        if when is None:
            copy.start()
        else:
            pl.when(when)(copy.start)

    def arrived(name, when=None):
        if when is None:
            copies[name].wait_recv()
        else:
            pl.when(when)(copies[name].wait_recv)

    filt_in = pltpu.make_async_copy(filt_ref, filtv, local.at[0])
    hy_in = pltpu.make_async_copy(hy_ref, hyv, local.at[1])
    ds_in = pltpu.make_async_copy(ds_ref, dsb.at[0, x], local.at[2])
    q_in = [
        pltpu.make_async_copy(q_ref.at[:, head_cols(x, h)], qb.at[h, 0, x], local.at[3 + h])
        for h in range(HEADS)
    ]
    kv_in = [
        pltpu.make_async_copy(kv_ref.at[:, :, head_cols(x, h)], kvb.at[h, ROW + x], local.at[5 + h])
        for h in range(HEADS)
    ]
    filt_in.start()
    for copy in q_in:
        copy.start()
    ds_in.start()
    hy_in.start()
    bias_in = pltpu.make_async_copy(bias_ref, biasv, local.at[8])
    bias_in.start()
    for copy in kv_in:
        copy.start()

    @pl.when(row == 0)
    def _():
        note = lax.broadcasted_iota(jnp.int32, (NOTE, BLK), 0)
        for h in range(HEADS):
            for s in range(ROW):
                came[1, h, s, pl.ds(0, HD), :] = jnp.zeros((HD, BLK), bf16)
                came[1, h, s, pl.ds(HD, NOTE), :] = jnp.where(note == 0, NONE, 0.0).astype(bf16)
        for h in range(HEADS):
            kvb[h, pl.ds(0, ROW)] = jnp.zeros((ROW, 2, BLK, HD), bf16)

    @pl.when(ctx == 0)
    def _():
        halo[...] = jnp.zeros_like(halo)

    pl.semaphore_wait(barrier, greetings)
    for other in range(tp_count - 1):

        @pl.when(other < tp)
        def _():
            pl.semaphore_signal(
                ready.at[tp], inc=1, device_id=(holder(other), other), device_id_type=MESH
            )

    def slot(d):
        return (x + ROW - d) % ROW

    def send_queries(h):
        for d in (1, 3, 2):
            cols = head_cols((x + d) % ROW, h)
            remote(("q", h, d), q_ref.at[:, cols], qb.at[h, 0, x], (mate(d), tp))
        remote(("qd", h, 0), q_ref.at[:, head_cols(x, h)], qb.at[h, 1, x], (down, tp), has_down)

    def send_keys(h):
        for d in (1, 3, 2):
            cols = head_cols((x + d) % ROW, h)
            remote(("kv", h, d), kv_ref.at[:, :, cols], kvb.at[h, ROW + x], (mate(d), tp))
        remote(
            ("ku", h, 0),
            kv_ref.at[:, :, head_cols(x, h)],
            kvb.at[h, x],
            (up, tp),
            has_up & (x != 0),
        )

    def queries_down(h, d):
        arrived(("q", h, d))
        remote(("qd", h, d), qb.at[h, 0, slot(d)], qb.at[h, 1, slot(d)], (down, tp), has_down)

    def keys_up(h, d):
        arrived(("kv", h, d))
        remote(
            ("ku", h, d),
            kvb.at[h, ROW + slot(d)],
            kvb.at[h, slot(d)],
            (up, tp),
            has_up & (slot(d) != 0),
        )

    def late_taps(sibling):
        for d in range(1, tp_count):
            other = (tp + d) % tp_count
            here = (other // CORES == tp // CORES) == sibling

            @pl.when((other > tp) & here)
            def _():
                pl.semaphore_wait(ready.at[other], 1)
                copies[("tap", d)].start()

    send_queries(0)
    send_keys(0)
    for d in (1, 3, 2):
        remote(("ds", d), ds_ref, dsb.at[0, x], (mate(d), tp))
    filt_in.wait()
    filtb[...] = filtv[...].astype(bf16)
    own_taps = pl.ds(pl.multiple_of(tp * tap_rows, tap_rows), tap_rows)
    for d in range(1, tp_count):
        other = (tp + d) % tp_count
        cols = pl.ds(pl.multiple_of(other * ch, ch), ch)
        remote(("tap", d), filtb.at[:, cols], tapb.at[own_taps], (holder(other), other), other < tp)
        sending[("tap", d)] = None
    tap_in = pltpu.make_async_copy(
        filtb.at[:, pl.ds(pl.multiple_of(tp * ch, ch), ch)], tapb.at[own_taps], local.at[7]
    )
    tap_in.start()
    for d in (1, 3, 2):
        queries_down(0, d)
    ds_in.wait()
    for d in (1, 3, 2):
        arrived(("ds", d))
    remote("ds1", dsb.at[0], dsb.at[1], (down, tp), has_down)
    keys_up(0, 1)
    keys_up(0, 3)
    send_queries(1)
    keys_up(0, 2)
    send_keys(1)
    late_taps(True)

    hy_in.wait()
    product = (hyv[1].astype(f32) * hyv[2].astype(f32)).astype(bf16)
    prod[...] = product
    late[pl.ds(0, SHIFTS), :] = jnp.zeros((SHIFTS, ch), f32)
    late[pl.ds(SHIFTS, BLK), :] = product.astype(f32)
    for b in range(SHIFTS):
        lates[b] = late[pl.ds(SHIFTS - b, BLK), :]

    for d in (1, 3, 2):
        queries_down(1, d)
    for d in (1, 3, 2):
        keys_up(1, d)
    late_taps(False)
    remote("halo", prod, halo, (after, tp), ctx < ctx_count - 1)

    base = row * ROW * BLK
    scale = 1.0 / math.sqrt(HD)

    def attend(h, level, first):
        span = (2 * ROW - first) * BLK
        keys = kvb[h, pl.ds(first, 2 * ROW - first), 0].reshape(span, HD)
        values = kvb[h, pl.ds(first, 2 * ROW - first), 1].reshape(span, HD)
        queries = qb[h, level].reshape(ROW * BLK, HD)
        scores = lax.dot_general(
            keys, queries, (((1,), (1,)), ((), ())), preferred_element_type=f32
        )
        starts = jnp.concatenate([dsb[level, i] for i in range(ROW)], axis=1) - base
        places = lax.broadcasted_iota(jnp.int32, scores.shape, 0) + (first - ROW) * BLK
        allowed = places >= starts
        if level == 0:
            allowed = allowed & (places <= lax.broadcasted_iota(jnp.int32, scores.shape, 1))
        scores = jnp.where(allowed, scores * scale, NONE)
        top = jnp.max(scores, axis=0, keepdims=True)
        weights = jnp.exp(scores - top)
        total = jnp.sum(weights, axis=0, keepdims=True)
        mixed = lax.dot_general(
            values, weights.astype(bf16), (((0,), (0,)), ((), ())), preferred_element_type=f32
        )
        return mixed / total, top + jnp.log(total)

    def merged(mixed_a, logs_a, mixed_b, logs_b):
        top = jnp.maximum(logs_a, logs_b)
        share_a = jnp.exp(logs_a - top)
        share_b = jnp.exp(logs_b - top)
        total = share_a + share_b
        mixed = mixed_a * (share_a / total) + mixed_b * (share_b / total)
        return mixed, top + jnp.log(total)

    def stage(level, h, mixed, logs):
        first = logs.astype(bf16).astype(f32)
        second = (logs - first).astype(bf16).astype(f32)
        third = logs - first - second
        place = lax.broadcasted_iota(jnp.int32, (NOTE, BLK), 0)
        for i in range(ROW):
            cols = slice(i * BLK, (i + 1) * BLK)
            sent[level, h, i, pl.ds(0, HD), :] = mixed[:, cols].astype(bf16)
            terms = jnp.where(
                place == 0,
                first[:, cols],
                jnp.where(place == 1, second[:, cols], jnp.where(place == 2, third[:, cols], 0.0)),
            )
            sent[level, h, i, pl.ds(HD, NOTE), :] = terms.astype(bf16)

    def own_part(h):
        q_in[h].wait()
        kv_in[h].wait()
        stage(0, h, *attend(h, 0, ROW))
        for d in (1, 3, 2):
            to = (x + d) % ROW
            remote(("o0", h, d), sent.at[0, h, to], came.at[0, h, x], (mate(d), tp))
        came[0, h, x] = sent[0, h, x]

    def earlier_part(h):
        for d in range(ROW):
            arrived(("qd", h, d), has_up)
            arrived(("ku", h, d), has_down & (slot(d) != 0))

        @pl.when(has_up)
        def _():
            stage(1, h, *attend(h, 1, 1))

        for d in (0, 1, 3, 2):
            to = (x + d) % ROW
            remote(("o1", h, d), sent.at[1, h, to], came.at[1, h, x], (higher(d), tp), has_up)

    def finish(h, s):
        own, earlier = came[0, h, s], came[1, h, s]

        def logs_of(tile):
            note = tile[HD:].astype(f32)
            return note[0:1] + note[1:2] + note[2:3]

        mixed, logs = merged(
            own[:HD].astype(f32), logs_of(own), earlier[:HD].astype(f32), logs_of(earlier)
        )
        head = s * HEADS + h
        att_out[:, pl.ds(head * HD, HD)] = mixed.T.astype(bf16)
        lt_out[pl.ds(head, 1), :] = logs

    groups = BLK // SHIFTS

    def start_columns():
        return jnp.broadcast_to((dsb[0, x] - base).astype(f32), (BLK, BLK)).T

    def rows_at():
        return lax.broadcasted_iota(jnp.int32, (BLK, BLK), 0).astype(f32) + (x * BLK).astype(f32)

    def reach_tiles():
        reach = rows_at() - start_columns()
        return [reach[SHIFTS * k : SHIFTS * (k + 1)] for k in range(groups)]

    def add_taps(acc, source, lanes, lag_groups, rows_of, row_of, reach):
        for a in lag_groups:
            group_taps = taps[pl.ds(SHIFTS * a, SHIFTS), lanes]
            for b in range(SHIFTS):
                weight = jnp.broadcast_to(group_taps[b : b + 1], (SHIFTS, BLK))
                for k in rows_of(a):
                    term = source[b, pl.ds(SHIFTS * row_of(k, a), SHIFTS), lanes] * weight
                    if reach is not None:
                        term = jnp.where(reach[k] >= SHIFTS * a + b, term, 0.0)
                    acc[k] = acc[k] + term

    def late_terms(half, fresh):
        def tile(c, carry):
            lanes = pl.ds(pl.multiple_of(c * 128, 128), 128)
            rows = [pl.ds(SHIFTS * k, SHIFTS) for k in range(groups)]
            if fresh:
                acc = [jnp.zeros((SHIFTS, 128), f32) for _ in rows]
            else:
                acc = [convolved[r, lanes] for r in rows]
            lag_groups = range(half * groups // 2, (half + 1) * groups // 2)
            reach = reach_tiles()
            add_taps(
                acc, lates, lanes, lag_groups, lambda a: range(a, groups), lambda k, a: k - a, reach
            )
            for k, r in enumerate(rows):
                if fresh or k >= lag_groups[0]:
                    convolved[r, lanes] = acc[k]
            return carry

        lax.fori_loop(0, tiles, tile, 0)

    def late_pass(halves, fresh):
        for half in range(2):
            which = (tp // CORES == half) == halves

            @pl.when(which)
            def _():
                late_terms(half, fresh)

    def tap_half(half):
        rows = pl.ds(pl.multiple_of(half * FLEN // 2, FLEN // 2), FLEN // 2)
        taps[rows, :] = tapb[rows, :].astype(f32)

    def early_tile(c, carry):
        lanes = pl.ds(pl.multiple_of(c * 128, 128), 128)
        acc = [jnp.zeros((SHIFTS, 128), f32) for _ in range(groups)]
        add_taps(
            acc, earlys, lanes, range(groups), lambda a: range(a + 1), lambda k, a: groups + k - a, None
        )
        reaches_back = start_columns() < (x * BLK).astype(f32)
        total = jnp.where(reaches_back, jnp.concatenate(acc, axis=0), 0.0)
        total = convolved[:, lanes] + total
        total = biasv[:, lanes] * late[pl.ds(SHIFTS, BLK), lanes] + total
        hy_out[:, lanes] = (hyv[0, :, lanes].astype(f32) * total).astype(bf16)
        return carry

    tiles = ch // 128

    even = tp % CORES == 0
    tap_in.wait()
    pl.when(even)(copies[("tap", 3)].wait_recv)
    pl.when(jnp.logical_not(even))(copies[("tap", 1)].wait_recv)
    tap_half(tp // CORES)
    late_pass(True, True)
    own_part(0)
    own_part(1)
    arrived("ds1", has_up)
    earlier_part(0)
    earlier_part(1)
    arrived(("tap", 2))
    pl.when(even)(copies[("tap", 1)].wait_recv)
    pl.when(jnp.logical_not(even))(copies[("tap", 3)].wait_recv)
    tap_half(1 - tp // CORES)
    late_pass(False, False)
    arrived("halo", ctx > 0)
    first_start = start_columns()[0:1]
    for c in range(tiles):
        cols = slice(c * 128, (c + 1) * 128)
        within = rows_at() - BLK >= first_start
        early[pl.ds(0, BLK), cols] = jnp.where(within, halo[:, cols].astype(f32), 0.0)
    early[pl.ds(BLK, SHIFTS), :] = jnp.zeros((SHIFTS, ch), f32)
    for b in range(SHIFTS):
        earlys[b, pl.ds(SHIFTS, BLK), :] = early[pl.ds(SHIFTS - b, BLK), :]
    bias_in.wait()
    lax.fori_loop(0, tiles, early_tile, 0)
    for h in range(HEADS):
        for d in (1, 3, 2):
            arrived(("o0", h, d))
        for d in (0, 1, 3, 2):
            arrived(("o1", h, d), has_down)
        for s in range(ROW):
            finish(h, s)
    for name, copy in copies.items():
        if sending[name] is None:
            copy.wait_send()
        else:
            pl.when(sending[name])(copy.wait_send)


def local_part(ctx_count, tp_count, hyena_inputs, filters, skip_bias, queries, keys_values, doc_start):
    rows, ch = queries.shape
    heads = ch // HD
    hbm = pl.BlockSpec(memory_space=pltpu.HBM)
    vmem = pl.BlockSpec(memory_space=pltpu.VMEM)

    def in_hbm(array):
        return pltpu.with_memory_space_constraint(array, pltpu.HBM)

    bf16, f32 = jnp.bfloat16, jnp.float32
    return pl.pallas_call(
        functools.partial(kernel, ctx_count, tp_count),
        name="row_exchange",
        out_shape=(
            jax.ShapeDtypeStruct((rows, ch), bf16),
            jax.ShapeDtypeStruct((rows, ch), bf16),
            jax.ShapeDtypeStruct((heads, rows), f32),
        ),
        in_specs=[hbm] * 6,
        out_specs=(vmem, vmem, vmem),
        scratch_shapes=[
            pltpu.VMEM((HEADS, 2 * ROW, 2, BLK, HD), bf16),
            pltpu.VMEM((HEADS, 2, ROW, BLK, HD), bf16),
            pltpu.VMEM((2, ROW, 1, BLK), jnp.int32),
            pltpu.VMEM((2, HEADS, ROW, HD + NOTE, BLK), bf16),
            pltpu.VMEM((2, HEADS, ROW, HD + NOTE, BLK), bf16),
            pltpu.VMEM((3, BLK, ch), bf16),
            pltpu.VMEM(filters.shape, f32),
            pltpu.VMEM(filters.shape, bf16),
            pltpu.VMEM((FLEN, ch), bf16),
            pltpu.VMEM((FLEN, ch), f32),
            pltpu.VMEM((BLK, ch), bf16),
            pltpu.VMEM((BLK, ch), bf16),
            pltpu.VMEM((BLK + SHIFTS, ch), f32),
            pltpu.VMEM((SHIFTS + BLK, ch), f32),
            pltpu.VMEM((SHIFTS, BLK + SHIFTS, ch), f32),
            pltpu.VMEM((SHIFTS, BLK, ch), f32),
            pltpu.VMEM((BLK, ch), f32),
            pltpu.VMEM((1, ch), f32),
            pltpu.SemaphoreType.DMA((56,)),
            pltpu.SemaphoreType.DMA((56,)),
            pltpu.SemaphoreType.DMA((9,)),
            pltpu.SemaphoreType.REGULAR((tp_count,)),
        ],
        compiler_params=pltpu.CompilerParams(
            collective_id=0, has_side_effects=True, vmem_limit_bytes=40 * 2**20
        ),
    )(
        in_hbm(hyena_inputs),
        in_hbm(filters),
        in_hbm(skip_bias.reshape(1, ch)),
        in_hbm(queries),
        in_hbm(keys_values),
        in_hbm(doc_start.reshape(1, rows)),
    )


def solution(mesh):
    in_specs = (
        P(None, "ctx", "tp"),
        P("tp", None),
        P("tp"),
        P("ctx", "tp"),
        P(None, "ctx", "tp"),
        P("ctx"),
    )
    out_specs = (P("ctx", "tp"), P("ctx", "tp"), P("tp", "ctx"))
    part = functools.partial(local_part, mesh.shape["ctx"], mesh.shape["tp"])
    return jax.shard_map(part, mesh=mesh, in_specs=in_specs, out_specs=out_specs, check_vma=False)
```

```python
import functools
import math

import jax
import jax.numpy as jnp
from jax import lax
from jax.experimental import pallas as pl
from jax.experimental.pallas import tpu as pltpu
from jax.sharding import PartitionSpec as P

MESH = pl.DeviceIdType.MESH
HD = 128
FLEN = 128
ROW = 4
BLK = 128
CORES = 2
PLANES = 4
PARTNER = (2, 1, 3, 0)
HEADS = 2
SHIFTS = 8
NONE = -1e30
NOTE = 16


def kernel(
    ctx_count,
    tp_count,
    hy_ref,
    filt_ref,
    bias_ref,
    q_ref,
    kv_ref,
    ds_ref,
    hy_out,
    att_out,
    lt_out,
    kvb,
    qb,
    dsb,
    sent,
    came,
    hyv,
    filtv,
    filtb,
    tapb,
    taps,
    halo,
    prod,
    early,
    late,
    earlys,
    lates,
    convolved,
    biasv,
    send,
    recv,
    local,
    ready,
):
    ctx = lax.axis_index("ctx")
    tp = lax.axis_index("tp")
    x = ctx % ROW
    row = ctx // ROW
    row_count = ctx_count // ROW
    plane = ctx_count // PLANES
    has_up = row < row_count - 1
    has_down = row > 0
    up = ((row + 1) % row_count) * ROW + x
    down = ((row + row_count - 1) % row_count) * ROW + x
    after = (ctx + 1) % ctx_count
    ch = hy_ref.shape[2]
    tap_rows = filt_ref.shape[0]
    bf16, f32 = jnp.bfloat16, jnp.float32

    def mate(d):
        return row * ROW + (x + d) % ROW

    def head_cols(owner, h):
        return pl.ds(pl.multiple_of((owner * HEADS + h) * HD, HD), HD)

    level = ctx // plane
    low = tp < CORES
    partner = 0
    for mine in range(PLANES):
        theirs = jnp.where(low, PARTNER[mine], PARTNER.index(mine))
        partner = jnp.where(level == mine, theirs, partner)
    mirrored = partner * plane + ctx % plane

    def holder(other):
        return jnp.where(other // CORES == tp // CORES, ctx, mirrored)

    def higher(d):
        return ((row + 1) % row_count) * ROW + (x + d) % ROW

    def lower(d):
        return ((row + row_count - 1) % row_count) * ROW + (x + d) % ROW

    barrier = pltpu.get_barrier_semaphore()

    def greet(peer):
        pl.semaphore_signal(barrier, inc=1, device_id=peer, device_id_type=MESH)

    for d in range(1, ROW):
        greet((mate(d), tp))
    for other in range(1, tp_count):

        @pl.when(other > tp)
        def _():
            greet((holder(other), other))

    @pl.when(has_up)
    def _():
        for d in range(ROW):
            greet((higher(d), tp))

    @pl.when(has_down)
    def _():
        for d in range(ROW):
            greet((lower(d), tp))

    greetings = ROW - 1 + tp + ROW * (has_up.astype(jnp.int32) + has_down.astype(jnp.int32))

    copies = {}
    sending = {}

    def remote(name, src, dst, peer, when=None):
        index = len(copies)
        copy = pltpu.make_async_remote_copy(
            src_ref=src,
            dst_ref=dst,
            send_sem=send.at[index],
            recv_sem=recv.at[index],
            device_id=peer,
            device_id_type=MESH,
        )
        copies[name] = copy
        sending[name] = when
        if when is None:
            copy.start()
        else:
            pl.when(when)(copy.start)

    def arrived(name, when=None):
        if when is None:
            copies[name].wait_recv()
        else:
            pl.when(when)(copies[name].wait_recv)

    filt_in = pltpu.make_async_copy(filt_ref, filtv, local.at[0])
    hy_in = pltpu.make_async_copy(hy_ref, hyv, local.at[1])
    ds_in = pltpu.make_async_copy(ds_ref, dsb.at[0, x], local.at[2])
    q_in = [
        pltpu.make_async_copy(q_ref.at[:, head_cols(x, h)], qb.at[h, 0, x], local.at[3 + h])
        for h in range(HEADS)
    ]
    kv_in = [
        pltpu.make_async_copy(kv_ref.at[:, :, head_cols(x, h)], kvb.at[h, ROW + x], local.at[5 + h])
        for h in range(HEADS)
    ]
    filt_in.start()
    for copy in q_in:
        copy.start()
    ds_in.start()
    hy_in.start()
    bias_in = pltpu.make_async_copy(bias_ref, biasv, local.at[8])
    bias_in.start()
    for copy in kv_in:
        copy.start()

    @pl.when(row == 0)
    def _():
        note = lax.broadcasted_iota(jnp.int32, (NOTE, BLK), 0)
        for h in range(HEADS):
            for s in range(ROW):
                came[1, h, s, pl.ds(0, HD), :] = jnp.zeros((HD, BLK), bf16)
                came[1, h, s, pl.ds(HD, NOTE), :] = jnp.where(note == 0, NONE, 0.0).astype(bf16)
        for h in range(HEADS):
            kvb[h, pl.ds(0, ROW)] = jnp.zeros((ROW, 2, BLK, HD), bf16)

    @pl.when(ctx == 0)
    def _():
        halo[...] = jnp.zeros_like(halo)

    pl.semaphore_wait(barrier, greetings)
    for other in range(tp_count - 1):

        @pl.when(other < tp)
        def _():
            pl.semaphore_signal(
                ready.at[tp], inc=1, device_id=(holder(other), other), device_id_type=MESH
            )

    def slot(d):
        return (x + ROW - d) % ROW

    def send_queries(h):
        for d in (1, 3, 2):
            cols = head_cols((x + d) % ROW, h)
            remote(("q", h, d), q_ref.at[:, cols], qb.at[h, 0, x], (mate(d), tp))
        remote(("qd", h, 0), q_ref.at[:, head_cols(x, h)], qb.at[h, 1, x], (down, tp), has_down)

    def send_keys(h):
        for d in (1, 3, 2):
            cols = head_cols((x + d) % ROW, h)
            remote(("kv", h, d), kv_ref.at[:, :, cols], kvb.at[h, ROW + x], (mate(d), tp))
        remote(
            ("ku", h, 0),
            kv_ref.at[:, :, head_cols(x, h)],
            kvb.at[h, x],
            (up, tp),
            has_up & (x != 0),
        )

    def queries_down(h, d):
        arrived(("q", h, d))
        remote(("qd", h, d), qb.at[h, 0, slot(d)], qb.at[h, 1, slot(d)], (down, tp), has_down)

    def keys_up(h, d):
        arrived(("kv", h, d))
        remote(
            ("ku", h, d),
            kvb.at[h, ROW + slot(d)],
            kvb.at[h, slot(d)],
            (up, tp),
            has_up & (slot(d) != 0),
        )

    def late_taps(sibling):
        for d in range(1, tp_count):
            other = (tp + d) % tp_count
            here = (other // CORES == tp // CORES) == sibling

            @pl.when((other > tp) & here)
            def _():
                pl.semaphore_wait(ready.at[other], 1)
                copies[("tap", d)].start()

    send_queries(0)
    send_keys(0)
    for d in (1, 3, 2):
        remote(("ds", d), ds_ref, dsb.at[0, x], (mate(d), tp))
    filt_in.wait()
    filtb[...] = filtv[...].astype(bf16)
    own_taps = pl.ds(pl.multiple_of(tp * tap_rows, tap_rows), tap_rows)
    for d in range(1, tp_count):
        other = (tp + d) % tp_count
        cols = pl.ds(pl.multiple_of(other * ch, ch), ch)
        remote(("tap", d), filtb.at[:, cols], tapb.at[own_taps], (holder(other), other), other < tp)
        sending[("tap", d)] = None
    tap_in = pltpu.make_async_copy(
        filtb.at[:, pl.ds(pl.multiple_of(tp * ch, ch), ch)], tapb.at[own_taps], local.at[7]
    )
    tap_in.start()
    for d in (1, 3, 2):
        queries_down(0, d)
    ds_in.wait()
    for d in (1, 3, 2):
        arrived(("ds", d))
    remote("ds1", dsb.at[0], dsb.at[1], (down, tp), has_down)
    keys_up(0, 1)
    keys_up(0, 3)
    send_queries(1)
    keys_up(0, 2)
    send_keys(1)
    late_taps(True)

    hy_in.wait()
    product = (hyv[1].astype(f32) * hyv[2].astype(f32)).astype(bf16)
    prod[...] = product
    late[pl.ds(0, SHIFTS), :] = jnp.zeros((SHIFTS, ch), f32)
    late[pl.ds(SHIFTS, BLK), :] = product.astype(f32)
    for b in range(SHIFTS):
        lates[b] = late[pl.ds(SHIFTS - b, BLK), :]

    for d in (1, 3, 2):
        queries_down(1, d)
    for d in (1, 3, 2):
        keys_up(1, d)
    late_taps(False)

    base = row * ROW * BLK
    scale = 1.0 / math.sqrt(HD)

    def attend(h, level, first):
        span = (2 * ROW - first) * BLK
        keys = kvb[h, pl.ds(first, 2 * ROW - first), 0].reshape(span, HD)
        values = kvb[h, pl.ds(first, 2 * ROW - first), 1].reshape(span, HD)
        queries = qb[h, level].reshape(ROW * BLK, HD)
        scores = lax.dot_general(
            keys, queries, (((1,), (1,)), ((), ())), preferred_element_type=f32
        )
        starts = jnp.concatenate([dsb[level, i] for i in range(ROW)], axis=1) - base
        places = lax.broadcasted_iota(jnp.int32, scores.shape, 0) + (first - ROW) * BLK
        allowed = places >= starts
        if level == 0:
            allowed = allowed & (places <= lax.broadcasted_iota(jnp.int32, scores.shape, 1))
        scores = jnp.where(allowed, scores * scale, NONE)
        top = jnp.max(scores, axis=0, keepdims=True)
        weights = jnp.exp(scores - top)
        total = jnp.sum(weights, axis=0, keepdims=True)
        mixed = lax.dot_general(
            values, weights.astype(bf16), (((0,), (0,)), ((), ())), preferred_element_type=f32
        )
        return mixed / total, top + jnp.log(total)

    def merged(mixed_a, logs_a, mixed_b, logs_b):
        top = jnp.maximum(logs_a, logs_b)
        share_a = jnp.exp(logs_a - top)
        share_b = jnp.exp(logs_b - top)
        total = share_a + share_b
        mixed = mixed_a * (share_a / total) + mixed_b * (share_b / total)
        return mixed, top + jnp.log(total)

    def stage(level, h, mixed, logs):
        first = logs.astype(bf16).astype(f32)
        second = (logs - first).astype(bf16).astype(f32)
        third = logs - first - second
        place = lax.broadcasted_iota(jnp.int32, (NOTE, BLK), 0)
        for i in range(ROW):
            cols = slice(i * BLK, (i + 1) * BLK)
            sent[level, h, i, pl.ds(0, HD), :] = mixed[:, cols].astype(bf16)
            terms = jnp.where(
                place == 0,
                first[:, cols],
                jnp.where(place == 1, second[:, cols], jnp.where(place == 2, third[:, cols], 0.0)),
            )
            sent[level, h, i, pl.ds(HD, NOTE), :] = terms.astype(bf16)

    def own_part(h):
        q_in[h].wait()
        kv_in[h].wait()
        stage(0, h, *attend(h, 0, ROW))
        for d in (1, 3, 2):
            to = (x + d) % ROW
            remote(("o0", h, d), sent.at[0, h, to], came.at[0, h, x], (mate(d), tp))
        came[0, h, x] = sent[0, h, x]

    def earlier_part(h):
        for d in range(ROW):
            arrived(("qd", h, d), has_up)
            arrived(("ku", h, d), has_down & (slot(d) != 0))

        @pl.when(has_up)
        def _():
            stage(1, h, *attend(h, 1, 1))

        for d in (0, 1, 3, 2):
            to = (x + d) % ROW
            remote(("o1", h, d), sent.at[1, h, to], came.at[1, h, x], (higher(d), tp), has_up)

    def finish(h, s):
        own, earlier = came[0, h, s], came[1, h, s]

        def logs_of(tile):
            note = tile[HD:].astype(f32)
            return note[0:1] + note[1:2] + note[2:3]

        mixed, logs = merged(
            own[:HD].astype(f32), logs_of(own), earlier[:HD].astype(f32), logs_of(earlier)
        )
        head = s * HEADS + h
        att_out[:, pl.ds(head * HD, HD)] = mixed.T.astype(bf16)
        lt_out[pl.ds(head, 1), :] = logs

    groups = BLK // SHIFTS

    def start_columns():
        return jnp.broadcast_to((dsb[0, x] - base).astype(f32), (BLK, BLK)).T

    def rows_at():
        return lax.broadcasted_iota(jnp.int32, (BLK, BLK), 0).astype(f32) + (x * BLK).astype(f32)

    def reach_tiles():
        reach = rows_at() - start_columns()
        return [reach[SHIFTS * k : SHIFTS * (k + 1)] for k in range(groups)]

    def add_taps(acc, source, lanes, lag_groups, rows_of, row_of, reach):
        for a in lag_groups:
            group_taps = taps[pl.ds(SHIFTS * a, SHIFTS), lanes]
            for b in range(SHIFTS):
                weight = jnp.broadcast_to(group_taps[b : b + 1], (SHIFTS, BLK))
                for k in rows_of(a):
                    term = source[b, pl.ds(SHIFTS * row_of(k, a), SHIFTS), lanes] * weight
                    if reach is not None:
                        term = jnp.where(reach[k] >= SHIFTS * a + b, term, 0.0)
                    acc[k] = acc[k] + term

    def late_terms(half, fresh):
        def tile(c, carry):
            lanes = pl.ds(pl.multiple_of(c * 128, 128), 128)
            rows = [pl.ds(SHIFTS * k, SHIFTS) for k in range(groups)]
            if fresh:
                acc = [jnp.zeros((SHIFTS, 128), f32) for _ in rows]
            else:
                acc = [convolved[r, lanes] for r in rows]
            lag_groups = range(half * groups // 2, (half + 1) * groups // 2)
            reach = reach_tiles()
            add_taps(
                acc, lates, lanes, lag_groups, lambda a: range(a, groups), lambda k, a: k - a, reach
            )
            for k, r in enumerate(rows):
                if fresh or k >= lag_groups[0]:
                    convolved[r, lanes] = acc[k]
            return carry

        lax.fori_loop(0, tiles, tile, 0)

    def late_pass(halves, fresh):
        for half in range(2):
            which = (tp // CORES == half) == halves

            @pl.when(which)
            def _():
                late_terms(half, fresh)

    def tap_half(half):
        rows = pl.ds(pl.multiple_of(half * FLEN // 2, FLEN // 2), FLEN // 2)
        taps[rows, :] = tapb[rows, :].astype(f32)

    def early_tile(c, carry):
        lanes = pl.ds(pl.multiple_of(c * 128, 128), 128)
        acc = [jnp.zeros((SHIFTS, 128), f32) for _ in range(groups)]
        add_taps(
            acc, earlys, lanes, range(groups), lambda a: range(a + 1), lambda k, a: groups + k - a, None
        )
        reaches_back = start_columns() < (x * BLK).astype(f32)
        total = jnp.where(reaches_back, jnp.concatenate(acc, axis=0), 0.0)
        total = convolved[:, lanes] + total
        total = biasv[:, lanes] * late[pl.ds(SHIFTS, BLK), lanes] + total
        hy_out[:, lanes] = (hyv[0, :, lanes].astype(f32) * total).astype(bf16)
        return carry

    tiles = ch // 128

    own_part(0)
    own_part(1)
    remote("halo", prod, halo, (after, tp), ctx < ctx_count - 1)
    even = tp % CORES == 0
    tap_in.wait()
    pl.when(even)(copies[("tap", 3)].wait_recv)
    pl.when(jnp.logical_not(even))(copies[("tap", 1)].wait_recv)
    tap_half(tp // CORES)
    late_pass(True, True)
    arrived("ds1", has_up)
    earlier_part(0)
    earlier_part(1)
    arrived(("tap", 2))
    pl.when(even)(copies[("tap", 1)].wait_recv)
    pl.when(jnp.logical_not(even))(copies[("tap", 3)].wait_recv)
    tap_half(1 - tp // CORES)
    late_pass(False, False)
    arrived("halo", ctx > 0)
    first_start = start_columns()[0:1]
    for c in range(tiles):
        cols = slice(c * 128, (c + 1) * 128)
        within = rows_at() - BLK >= first_start
        early[pl.ds(0, BLK), cols] = jnp.where(within, halo[:, cols].astype(f32), 0.0)
    early[pl.ds(BLK, SHIFTS), :] = jnp.zeros((SHIFTS, ch), f32)
    for b in range(SHIFTS):
        earlys[b, pl.ds(SHIFTS, BLK), :] = early[pl.ds(SHIFTS - b, BLK), :]
    bias_in.wait()
    lax.fori_loop(0, tiles, early_tile, 0)
    for h in range(HEADS):
        for d in (1, 3, 2):
            arrived(("o0", h, d))
        for d in (0, 1, 3, 2):
            arrived(("o1", h, d), has_down)
        for s in range(ROW):
            finish(h, s)
    for name, copy in copies.items():
        if sending[name] is None:
            copy.wait_send()
        else:
            pl.when(sending[name])(copy.wait_send)


def local_part(ctx_count, tp_count, hyena_inputs, filters, skip_bias, queries, keys_values, doc_start):
    rows, ch = queries.shape
    heads = ch // HD
    hbm = pl.BlockSpec(memory_space=pltpu.HBM)
    vmem = pl.BlockSpec(memory_space=pltpu.VMEM)

    def in_hbm(array):
        return pltpu.with_memory_space_constraint(array, pltpu.HBM)

    bf16, f32 = jnp.bfloat16, jnp.float32
    return pl.pallas_call(
        functools.partial(kernel, ctx_count, tp_count),
        name="row_exchange",
        out_shape=(
            jax.ShapeDtypeStruct((rows, ch), bf16),
            jax.ShapeDtypeStruct((rows, ch), bf16),
            jax.ShapeDtypeStruct((heads, rows), f32),
        ),
        in_specs=[hbm] * 6,
        out_specs=(vmem, vmem, vmem),
        scratch_shapes=[
            pltpu.VMEM((HEADS, 2 * ROW, 2, BLK, HD), bf16),
            pltpu.VMEM((HEADS, 2, ROW, BLK, HD), bf16),
            pltpu.VMEM((2, ROW, 1, BLK), jnp.int32),
            pltpu.VMEM((2, HEADS, ROW, HD + NOTE, BLK), bf16),
            pltpu.VMEM((2, HEADS, ROW, HD + NOTE, BLK), bf16),
            pltpu.VMEM((3, BLK, ch), bf16),
            pltpu.VMEM(filters.shape, f32),
            pltpu.VMEM(filters.shape, bf16),
            pltpu.VMEM((FLEN, ch), bf16),
            pltpu.VMEM((FLEN, ch), f32),
            pltpu.VMEM((BLK, ch), bf16),
            pltpu.VMEM((BLK, ch), bf16),
            pltpu.VMEM((BLK + SHIFTS, ch), f32),
            pltpu.VMEM((SHIFTS + BLK, ch), f32),
            pltpu.VMEM((SHIFTS, BLK + SHIFTS, ch), f32),
            pltpu.VMEM((SHIFTS, BLK, ch), f32),
            pltpu.VMEM((BLK, ch), f32),
            pltpu.VMEM((1, ch), f32),
            pltpu.SemaphoreType.DMA((56,)),
            pltpu.SemaphoreType.DMA((56,)),
            pltpu.SemaphoreType.DMA((9,)),
            pltpu.SemaphoreType.REGULAR((tp_count,)),
        ],
        compiler_params=pltpu.CompilerParams(
            collective_id=0, has_side_effects=True, vmem_limit_bytes=40 * 2**20
        ),
    )(
        in_hbm(hyena_inputs),
        in_hbm(filters),
        in_hbm(skip_bias.reshape(1, ch)),
        in_hbm(queries),
        in_hbm(keys_values),
        in_hbm(doc_start.reshape(1, rows)),
    )


def solution(mesh):
    in_specs = (
        P(None, "ctx", "tp"),
        P("tp", None),
        P("tp"),
        P("ctx", "tp"),
        P(None, "ctx", "tp"),
        P("ctx"),
    )
    out_specs = (P("ctx", "tp"), P("ctx", "tp"), P("tp", "ctx"))
    part = functools.partial(local_part, mesh.shape["ctx"], mesh.shape["tp"])
    return jax.shard_map(part, mesh=mesh, in_specs=in_specs, out_specs=out_specs, check_vma=False)
```
